256 devices in a mesh: dp: 16 (over z, core), tensor: 16 (over y, x).
Axes of the slice: x: 4, y: 4, z: 8, core: 2. Of those that a mesh axis runs over, the one named last changes fastest.
Arguments:
- tokens: bfloat16 [8192, 8192], P('dp', 'tensor'), may hold values from -6 to 6
- grad_out: bfloat16 [8192, 28672], P('dp', 'tensor'), may hold values from -0.06591797 to 0.06591797
- projector: bfloat16 [8192, 1024], P('tensor'), may hold values from -0.1875 to 0.1875
- weight: float32 [8192, 28672], P('dp', 'tensor'), may hold values from -6 to 6
- first_moment: float32 [1024, 28672], P('dp', 'tensor'), may hold values from -6 to 6
- second_moment: float32 [1024, 28672], P('dp', 'tensor'), may hold values from 0.5 to 4
Outputs:
- new_weight: float32 [8192, 28672], P('dp', 'tensor')
- new_first: float32 [1024, 28672], P('dp', 'tensor')
- new_second: float32 [1024, 28672], P('dp', 'tensor')
The draws below stay inside these ranges and needn't reach their ends.
All inputs are finite; a program needn't handle non-finite values.
Results may differ from the reference program's by a relative error of at most 0.00098.
Values may be sent and summed in bfloat16 or wider, within the bound.
A program may use at most 64 MiB of HBM per device.

```python
import math
import jax
import jax.numpy as jnp
from jax import lax

D = 8192
FF = 28672
R = 1024
STEP = 1000
TOKENS = 8192


def levels(key, dims, pieces, smallest, top_value):
    loudness, own = 1.0, jax.random.fold_in(key, 6)
    for axis_at, blocks in pieces:
        heights = jnp.exp(jax.random.uniform(jax.random.fold_in(own, axis_at), (blocks,), jnp.float32, smallest / len(pieces), top_value / len(pieces)))
        loudness = loudness * jnp.repeat(heights, dims[axis_at] // blocks).reshape([-1 if axis == axis_at else 1 for axis in range(len(dims))])
    return loudness


def gaussian(key, dims, scale, most, cuts=(), kind=jnp.bfloat16):
    level = levels(key, dims, cuts, -0.22, 0.18) if cuts else 1.0
    result = jax.random.normal(key, dims, jnp.float32) * scale * level
    return jnp.minimum(jnp.maximum(result, -most), most).astype(kind)


def setup_inputs(seed: int = 0) -> dict:
    key_list = jax.random.split(jax.random.key(seed), 7)
    return {
        "tokens": gaussian(key_list[0], (TOKENS, D), 1.0, 6.0, ((0, 16), (1, 16))),
        "grad_out": gaussian(key_list[1], (TOKENS, FF), (1.0 * TOKENS ** -0.5), 0.06591797, ((0, 16), (1, 16))),
        "projector": gaussian(key_list[2], (D, R), R ** -0.5, 0.1875, ((0, 16),)),
        "weight": gaussian(key_list[3], (D, FF), 1.0, 6.0, ((0, 16), (1, 16)), jnp.float32),
        "first_moment": gaussian(key_list[4], (R, FF), 1.0, 6.0, ((0, 16), (1, 16)), jnp.float32),
        "second_moment": jnp.clip(jnp.exp(math.log(4.0) - 2.0794415 * jax.random.uniform(key_list[5], (R, FF), jnp.float32) ** levels(key_list[5], (R, FF), ((0, 16), (1, 16)), -0.2, 0.2)), 0.5, 4.0),
    }


def reference(tokens, grad_out, projector, weight, first_moment, second_moment):
    projected = jnp.dot(tokens, projector, preferred_element_type=jnp.float32).astype(jnp.bfloat16)
    grad = lax.dot_general(projected, grad_out, (((0,), (0,)), ((), ())), preferred_element_type=jnp.float32)
    new_first = 0.9 * first_moment + 0.1 * grad
    new_second = 0.999 * second_moment + 0.001 * grad * grad
    first_fix = 1.0 - 0.9 ** STEP
    second_fix = 1.0 - 0.999 ** STEP
    direction = (new_first / first_fix / (jnp.sqrt(new_second / second_fix) + 1e-08)).astype(jnp.bfloat16)
    new_weight = weight - 0.5 * jnp.dot(projector, direction, preferred_element_type=jnp.float32)
    return (new_weight, new_first, new_second)
```

```python
import functools

import jax
import jax.numpy as jnp
from jax import lax
from jax.experimental import pallas as pl
from jax.experimental.pallas import tpu as pltpu
from jax.sharding import PartitionSpec as P

STEP = 1000
MESH = pl.DeviceIdType.MESH
F32, BF16 = jnp.float32, jnp.bfloat16
K = 4
NZ, NY, NX = 8, 4, 4
ROWS = 64
RB = ROWS // K
NR = NZ * RB
FFL = 1792
HALF = FFL // 2
TILE = 256
OFFSET = 2
PEERS = NY * NX


def kernel(
    tokens, grad_out, projector, weight, first, second,
    out_w, out_first, out_second,
    tok_v, go_v, proj_v, first_v, second_v, pick, pc, part, r1, s1, r2, pj, pjt, gp,
    zs, zr, dir_v, held, hp,
    load_sem, tok_sem, go_sem, x1_sem, x2_sem, pg_sem, z_sem, a_sem, sib_sem, sc_sem, hg_sem,
):
    dp, t = lax.axis_index("dp"), lax.axis_index("tensor")
    z, c = dp // 2, dp % 2
    y, x = t // NX, t % NX

    def at(dz=0, dy=0, dx=0):
        return (lax.rem(z + dz + NZ, NZ) * 2 + c, lax.rem(y + dy, NY) * NX + lax.rem(x + dx, NX))

    sibling = (2 * z + 1 - c, t)

    def plane_peer(j):
        return at(0, j // NX, j % NX)

    def remote(src, dst, sems, idx, device):
        send, recv = sems
        return pltpu.make_async_remote_copy(
            src_ref=src, dst_ref=dst, send_sem=send.at[idx], recv_sem=recv.at[idx],
            device_id=device, device_id_type=MESH,
        )

    barrier = pltpu.get_barrier_semaphore()
    for dz in (1, -1):
        pl.semaphore_signal(barrier, inc=1, device_id=at(dz), device_id_type=MESH)
    pl.semaphore_signal(barrier, inc=1, device_id=sibling, device_id_type=MESH)

    @pl.loop(1, PEERS)
    def _(j):
        pl.semaphore_signal(barrier, inc=1, device_id=plane_peer(j), device_id_type=MESH)

    loads = [
        pltpu.make_async_copy(projector, proj_v, load_sem.at[0]),
        pltpu.make_async_copy(tokens, tok_v.at[c], load_sem.at[1]),
        pltpu.make_async_copy(grad_out, go_v.at[:, c], load_sem.at[2]),
        pltpu.make_async_copy(first, first_v, load_sem.at[3]),
        pltpu.make_async_copy(second, second_v, load_sem.at[4]),
        pltpu.make_async_copy(weight, out_w, load_sem.at[5]),
    ]
    for copy in loads:
        copy.start()

    @pl.loop(0, NZ)
    def _(b):
        row = lax.broadcasted_iota(jnp.int32, (2 * ROWS, K * NR), 0)
        col = lax.broadcasted_iota(jnp.int32, (2 * ROWS, K * NR), 1)
        chunk, in_chunk = col // NR, col % NR
        plane, r = in_chunk // RB, in_chunk % RB
        for cc in range(2):
            hit = (plane == b) & (row == cc * ROWS + chunk * RB + r)
            pick[cc, pl.ds(pl.multiple_of(b * 2 * ROWS, 2 * ROWS), 2 * ROWS), :] = jnp.where(
                hit, 1.0, 0.0
            ).astype(BF16)

    loads[0].wait()
    pc[...] = jnp.dot(proj_v[...], pick[c], preferred_element_type=F32).astype(BF16)
    loads[1].wait()

    def partial_product(h):
        @pl.loop(0, NY)
        def _(yy):
            rows = pl.ds(pl.multiple_of(yy * 128, 128), 128)
            value = jnp.dot(tok_v[h, rows, :], pc[...], preferred_element_type=F32)
            for k in range(K):
                part[k, h, yy] = value[:, k * NR : (k + 1) * NR].reshape(NX, 32, NR)

    partial_product(c)

    pl.semaphore_wait(barrier, 2 + 1 + PEERS - 1)
    tok_copy = remote(tok_v.at[c], tok_v.at[c], tok_sem, 0, sibling)
    go_copy = remote(grad_out, go_v.at[:, c], go_sem, 0, sibling)
    tok_copy.start()
    go_copy.start()

    def x1(k, h, i):
        if h == 0:
            return remote(
                part.at[k, 0, :, lax.rem(x + i, NX)], r1.at[k, 0, i - 1], x1_sem,
                (k * 2 + h) * 3 + i - 1, at(0, 0, i),
            )
        return remote(
            part.at[k, 1, lax.rem(y + i, NY)], r1.at[k, 1, i - 1], x1_sem,
            (k * 2 + h) * 3 + i - 1, at(0, i, 0),
        )

    def x2(k, h, i):
        if h == 0:
            return remote(
                s1.at[k, 0, lax.rem(y + i, NY)], r2.at[k, 0, i - 1], x2_sem,
                (k * 2 + h) * 3 + i - 1, at(0, i, 0),
            )
        return remote(
            s1.at[k, 1, lax.rem(x + i, NX)], r2.at[k, 1, i - 1], x2_sem,
            (k * 2 + h) * 3 + i - 1, at(0, 0, i),
        )

    def plane_gather(k, j):
        return remote(pj.at[k, t], pj.at[k, t], pg_sem, k * PEERS + j, plane_peer(j))

    def z_step(k, d, s):
        cols = pl.ds(d * HALF, HALF) if s == 0 else pl.ds(0, FFL)
        return remote(
            zs.at[k, d, s, :, cols], zr.at[k, d, s, :, cols], z_sem, (k * 2 + d) * 4 + s,
            at(1 if d == 0 else -1),
        )

    def a_step(k, d, s):
        piece = lax.rem(z + (NZ - s if d == 0 else s), NZ)
        cols = pl.ds(d * HALF, HALF) if s == 3 else pl.ds(0, FFL)
        ref = dir_v.at[k, c, piece, :, cols]
        return remote(ref, ref, a_sem, (k * 2 + d) * 4 + s, at(1 if d == 0 else -1))

    def sib(k, n):
        ref = dir_v.at[k, c, lax.rem(z + NZ - n, NZ)]
        return remote(ref, ref, sib_sem, k * NZ + n, sibling)

    def stage_x1(k):
        for h in range(2):
            for i in (1, 2, 3):
                x1(k, h, i).start()

    def stage_x2(k):
        for h in range(2):
            for i in (1, 2, 3):
                x1(k, h, i).wait_recv()
            own = part[k, 0, :, pl.ds(x, 1)].reshape(NY, 32, NR) if h == 0 else part[k, 1, y]
            s1[k, h] = own + r1[k, h, 0] + r1[k, h, 1] + r1[k, h, 2]
            for i in (1, 2, 3):
                x2(k, h, i).start()

    def stage_pg(k):
        for h in range(2):
            for i in (1, 2, 3):
                x2(k, h, i).wait_recv()
            own = s1[k, h, y if h == 0 else x]
            pj[k, t, h] = (own + r2[k, h, 0] + r2[k, h, 1] + r2[k, h, 2]).astype(BF16)

        @pl.loop(1, PEERS)
        def _(j):
            plane_gather(k, j).start()

    def stage_grad(k):
        @pl.loop(1, PEERS)
        def _(j):
            plane_gather(k, j).wait_recv()

        if k == 0:
            loads[2].wait()
            go_copy.wait_recv()
        pjt[...] = pj[k].reshape(PEERS * 64, NR).T

        @pl.loop(0, FFL // TILE)
        def _(n):
            cols = pl.ds(pl.multiple_of(n * TILE, TILE), TILE)
            value = jnp.dot(
                pjt[...], go_v[:, :, :, cols].reshape(PEERS * 64, TILE), preferred_element_type=F32
            )
            gp[k, :, :, cols] = value.reshape(NZ, RB, TILE)

        for d in range(2):
            far = lax.rem(z + 4, NZ)
            cols = slice(d * HALF, (d + 1) * HALF)
            zs[k, d, 0, :, cols] = gp[k, far, :, cols].astype(BF16)
            z_step(k, d, 0).start()

    def stage_z(k, s):
        for d in range(2):
            z_step(k, d, s - 1).wait_recv()
            dest = lax.rem(z + (4 - s if d == 0 else NZ - 4 + s), NZ)
            if s == 1:
                got = slice(d * HALF, (d + 1) * HALF)
                rest = slice((1 - d) * HALF, (2 - d) * HALF)
                zs[k, d, 1, :, got] = (
                    gp[k, dest, :, got] + zr[k, d, 0, :, got].astype(F32)
                ).astype(BF16)
                zs[k, d, 1, :, rest] = gp[k, dest, :, rest].astype(BF16)
            else:
                zs[k, d, s] = (gp[k, dest] + zr[k, d, s - 1].astype(F32)).astype(BF16)
            z_step(k, d, s).start()

    def stage_adam(k):
        for d in range(2):
            z_step(k, d, 3).wait_recv()
        if k == 0:
            loads[3].wait()
            loads[4].wait()
        rows = slice(k * RB, (k + 1) * RB)
        grad = gp[k, z] + zr[k, 0, 3].astype(F32) + zr[k, 1, 3].astype(F32)
        new_first = 0.9 * first_v[rows, :] + 0.1 * grad
        new_second = 0.999 * second_v[rows, :] + 0.001 * grad * grad
        out_first[rows, :] = new_first
        out_second[rows, :] = new_second
        first_fix = 1.0 - 0.9**STEP
        second_fix = 1.0 - 0.999**STEP
        dir_v[k, c, z] = (
            new_first / first_fix / (jnp.sqrt(new_second / second_fix) + 1e-08)
        ).astype(BF16)
        for d in range(2):
            a_step(k, d, 0).start()
        sib(k, 0).start()

    def stage_a(k, s):
        for d in range(2):
            a_step(k, d, s - 1).wait_recv()
            a_step(k, d, s).start()
            sib(k, s if d == 0 else NZ - s).start()

    def stage_last(k):
        for d in range(2):
            a_step(k, d, 3).wait_recv()
        sib(k, 4).start()

    def stage_product(k):
        for n in range(NZ):
            sib(k, n).wait_recv()

        @pl.loop(0, FFL // TILE)
        def _(n):
            cols = pl.ds(pl.multiple_of(n * TILE, TILE), TILE)
            value = jnp.dot(
                hp[:, k * 2 * NR : (k + 1) * 2 * NR],
                dir_v[k, :, :, :, cols].reshape(2 * NR, TILE),
                preferred_element_type=F32,
            )
            out_w[:, cols] = out_w[:, cols] - 0.5 * value

    holder = dp
    is_holder = t == holder

    def piece_of(ref, p):
        return ref.at[pl.ds(pl.multiple_of(p * 32, 32), 32)]

    def scatter(p):
        return pltpu.make_async_remote_copy(
            src_ref=piece_of(proj_v, p), dst_ref=piece_of(held, p),
            send_sem=sc_sem[0].at[p], recv_sem=sc_sem[1].at[0],
            device_id=(dp, p), device_id_type=MESH,
        )

    def held_gather(j):
        return remote(piece_of(held, t), piece_of(held, t), hg_sem, j, plane_peer(j))

    def own_held():
        return pltpu.make_async_copy(proj_v, held, load_sem.at[6])

    def stage_scatter():
        @pl.when(is_holder)
        def _():
            own_held().start()

            @pl.loop(1, PEERS)
            def _(j):
                scatter(lax.rem(t + j, PEERS)).start()

    def stage_held_gather():
        @pl.when(is_holder)
        def _():
            own_held().wait()

        @pl.when(jnp.logical_not(is_holder))
        def _():
            scatter(t).wait_recv()

        @pl.loop(1, PEERS)
        def _(j):
            @pl.when(plane_peer(j)[1] != holder)
            def _():
                held_gather(j).start()

    def stage_held():
        @pl.when(jnp.logical_not(is_holder))
        def _():
            @pl.loop(1, PEERS)
            def _(j):
                held_gather(j).wait_recv()

        for cc in range(2):
            @pl.loop(0, 4)
            def _(b):
                rows = pl.ds(pl.multiple_of(b * 128, 128), 128)
                value = jnp.dot(held[rows, :], pick[cc], preferred_element_type=F32).astype(BF16)
                for k in range(K):
                    lo = (k * 2 + cc) * NR
                    hp[rows, lo : lo + NR] = value[:, k * NR : (k + 1) * NR]

        loads[5].wait()

    tok_copy.wait_recv()
    partial_product(1 - c)

    stages = [
        stage_x1, stage_x2, stage_pg, stage_grad,
        functools.partial(lambda s, k: stage_z(k, s), 1),
        functools.partial(lambda s, k: stage_z(k, s), 2),
        functools.partial(lambda s, k: stage_z(k, s), 3),
        stage_adam,
        functools.partial(lambda s, k: stage_a(k, s), 1),
        functools.partial(lambda s, k: stage_a(k, s), 2),
        functools.partial(lambda s, k: stage_a(k, s), 3),
        stage_last, stage_product,
    ]
    for slot in range(len(stages) + OFFSET * (K - 1)):
        if slot == 5:
            stage_scatter()
        if slot == 8:
            stage_held_gather()
        if slot == 11:
            stage_held()
        for k in range(K):
            n = slot - OFFSET * k
            if 0 <= n < len(stages):
                stages[n](k)

    tok_copy.wait_send()
    go_copy.wait_send()
    for k in range(K):
        for h in range(2):
            for i in (1, 2, 3):
                x1(k, h, i).wait_send()
                x2(k, h, i).wait_send()
            for s in range(4):
                z_step(k, h, s).wait_send()
                a_step(k, h, s).wait_send()
        for n in range(NZ):
            sib(k, n).wait_send()

        @pl.loop(1, PEERS)
        def _(j):
            plane_gather(k, j).wait_send()

    @pl.loop(1, PEERS)
    def _(j):
        @pl.when(plane_peer(j)[1] != holder)
        def _():
            held_gather(j).wait_send()

    @pl.when(is_holder)
    def _():
        @pl.loop(1, PEERS)
        def _(j):
            scatter(lax.rem(t + j, PEERS)).wait_send()


def on_device(tokens, grad_out, projector, weight, first_moment, second_moment):
    dma = pltpu.SemaphoreType.DMA

    def pair(n):
        return [dma((n,)), dma((n,))]

    scratch = [
        pltpu.VMEM((2, 512, 512), BF16),
        pltpu.VMEM((PEERS, 2, 32, FFL), BF16),
        pltpu.VMEM((512, 1024), BF16),
        pltpu.VMEM((ROWS, FFL), F32),
        pltpu.VMEM((ROWS, FFL), F32),
        pltpu.VMEM((2, 1024, K * NR), BF16),
        pltpu.VMEM((512, K * NR), BF16),
        pltpu.VMEM((K, 2, NY, NX, 32, NR), F32),
        pltpu.VMEM((K, 2, 3, 4, 32, NR), F32),
        pltpu.VMEM((K, 2, 4, 32, NR), F32),
        pltpu.VMEM((K, 2, 3, 32, NR), F32),
        pltpu.VMEM((K, PEERS, 2, 32, NR), BF16),
        pltpu.VMEM((NR, PEERS * 64), BF16),
        pltpu.VMEM((K, NZ, RB, FFL), F32),
        pltpu.VMEM((K, 2, 4, RB, FFL), BF16),
        pltpu.VMEM((K, 2, 4, RB, FFL), BF16),
        pltpu.VMEM((K, 2, NZ, RB, FFL), BF16),
        pltpu.VMEM((512, 1024), BF16),
        pltpu.VMEM((512, 1024), BF16),
        dma((7,)),
        pair(1), pair(1), pair(K * 6), pair(K * 6), pair(K * PEERS), pair(K * 8), pair(K * 8),
        pair(K * NZ), pair(PEERS), pair(PEERS),
    ]
    any_spec = pl.BlockSpec(memory_space=pl.ANY)
    vmem_spec = pl.BlockSpec(memory_space=pltpu.VMEM)
    return pl.pallas_call(
        kernel,
        out_shape=(
            jax.ShapeDtypeStruct(weight.shape, F32),
            jax.ShapeDtypeStruct(first_moment.shape, F32),
            jax.ShapeDtypeStruct(second_moment.shape, F32),
        ),
        in_specs=[any_spec] * 6,
        out_specs=[vmem_spec] * 3,
        scratch_shapes=scratch,
        compiler_params=pltpu.CompilerParams(
            collective_id=0, has_side_effects=True, vmem_limit_bytes=56 * 2**20
        ),
        cost_estimate=pl.CostEstimate(
            flops=6 * 10**9, bytes_accessed=13 * 2**20, transcendentals=0
        ),
    )(tokens, grad_out.reshape(PEERS, 32, FFL), projector, weight, first_moment, second_moment)


def solution(mesh):
    spec = P("dp", "tensor")
    in_specs = (spec, spec, P("tensor", None), spec, spec, spec)
    return jax.shard_map(
        on_device, mesh=mesh, in_specs=in_specs, out_specs=(spec, spec, spec), check_vma=False
    )
```

```python
import functools

import jax
import jax.numpy as jnp
from jax import lax
from jax.experimental import pallas as pl
from jax.experimental.pallas import tpu as pltpu
from jax.sharding import PartitionSpec as P

STEP = 1000
MESH = pl.DeviceIdType.MESH
F32, BF16 = jnp.float32, jnp.bfloat16
K = 4
NZ, NY, NX = 8, 4, 4
ROWS = 64
RB = ROWS // K
NR = NZ * RB
FFL = 1792
HALF = FFL // 2
PEERS = NY * NX

ORDER = (
    (0, 0), (0, 1), (0, 2), (0, 3), (1, 0), (1, 1), (1, 2), (1, 3), (2, 0), (2, 1), (2, 2), (2, 3), "scatter",
    (3, 0), (3, 1), (4, 0), (3, 2), (4, 1), (5, 0), (3, 3), (4, 2), (5, 1), (6, 0), (4, 3), "gather", (5, 2),
    (6, 1), (7, 0), (5, 3), (6, 2), (7, 1), (8, 0), (6, 3), (7, 2), (8, 1), (9, 0), (7, 3), "held", (8, 2),
    (9, 1), (10, 0), (8, 3), (9, 2), (10, 1), (11, 0), (12, 0), (9, 3), (10, 2), (11, 1), (12, 1), (10, 3),
    (11, 2), (12, 2), (11, 3), (12, 3),
)


def kernel(
    tokens, grad_out, projector, weight, first, second,
    out_w, out_first, out_second,
    tok_v, go_v, proj_v, first_v, second_v, pick, pc, part, r1, s1, r2, pj, pjt, gp,
    zs, zr, dir_v, held, hp,
    load_sem, tok_sem, go_sem, x1_sem, x2_sem, pg_sem, z_sem, a_sem, sib_sem, sc_sem, hg_sem,
):
    dp, t = lax.axis_index("dp"), lax.axis_index("tensor")
    z, c = dp // 2, dp % 2
    y, x = t // NX, t % NX

    def at(dz=0, dy=0, dx=0):
        return (lax.rem(z + dz + NZ, NZ) * 2 + c, lax.rem(y + dy, NY) * NX + lax.rem(x + dx, NX))

    sibling = (2 * z + 1 - c, t)

    def plane_peer(j):
        return at(0, j // NX, j % NX)

    def remote(src, dst, sems, idx, device):
        send, recv = sems
        return pltpu.make_async_remote_copy(
            src_ref=src, dst_ref=dst, send_sem=send.at[idx], recv_sem=recv.at[idx],
            device_id=device, device_id_type=MESH,
        )

    drains = []

    def start(copy):
        copy.start()
        drains.append(copy.wait_send)

    barrier = pltpu.get_barrier_semaphore()
    for dz in (1, -1):
        pl.semaphore_signal(barrier, inc=1, device_id=at(dz), device_id_type=MESH)
    pl.semaphore_signal(barrier, inc=1, device_id=sibling, device_id_type=MESH)

    @pl.loop(1, PEERS)
    def _(j):
        pl.semaphore_signal(barrier, inc=1, device_id=plane_peer(j), device_id_type=MESH)

    loads = [
        pltpu.make_async_copy(projector, proj_v, load_sem.at[0]),
        pltpu.make_async_copy(tokens, tok_v.at[c], load_sem.at[1]),
        pltpu.make_async_copy(grad_out, go_v.at[:, c], load_sem.at[2]),
        pltpu.make_async_copy(first, first_v, load_sem.at[3]),
        pltpu.make_async_copy(second, second_v, load_sem.at[4]),
        pltpu.make_async_copy(weight, out_w, load_sem.at[5]),
    ]
    for copy in loads:
        copy.start()

    col = lax.broadcasted_iota(jnp.int32, (1, K * NR), 1)
    natural = col // RB % NZ * (2 * ROWS) + col // NR * RB + col % RB

    @pl.loop(0, NZ)
    def _(b):
        row = lax.broadcasted_iota(jnp.int32, (2 * ROWS, K * NR), 0)
        for cc in range(2):
            hit = row == natural + (cc * ROWS - b * (2 * ROWS))
            pick[cc, pl.ds(pl.multiple_of(b * 2 * ROWS, 2 * ROWS), 2 * ROWS), :] = jnp.where(
                hit, 1.0, 0.0
            ).astype(BF16)

    loads[0].wait()
    pc[...] = jnp.dot(proj_v[...], pick[c], preferred_element_type=F32).astype(BF16)
    loads[1].wait()

    def partial_product(h):
        value = jnp.dot(tok_v[h], pc[...], preferred_element_type=F32)
        for k in range(K):
            part[k, h] = value[:, k * NR : (k + 1) * NR].reshape(NY, NX, 32, NR)

    partial_product(c)

    pl.semaphore_wait(barrier, 2 + 1 + PEERS - 1)
    tok_copy = remote(tok_v.at[c], tok_v.at[c], tok_sem, 0, sibling)
    go_copy = remote(grad_out, go_v.at[:, c], go_sem, 0, sibling)
    start(tok_copy)
    start(go_copy)

    def x1(k, h, i):
        if h == 0:
            return remote(
                part.at[k, 0, :, lax.rem(x + i, NX)], r1.at[k, 0, i - 1], x1_sem,
                (k * 2 + h) * 3 + i - 1, at(0, 0, i),
            )
        return remote(
            part.at[k, 1, lax.rem(y + i, NY)], r1.at[k, 1, i - 1], x1_sem,
            (k * 2 + h) * 3 + i - 1, at(0, i, 0),
        )

    def x2(k, h, i):
        if h == 0:
            return remote(
                s1.at[k, 0, lax.rem(y + i, NY)], r2.at[k, 0, i - 1], x2_sem,
                (k * 2 + h) * 3 + i - 1, at(0, i, 0),
            )
        return remote(
            s1.at[k, 1, lax.rem(x + i, NX)], r2.at[k, 1, i - 1], x2_sem,
            (k * 2 + h) * 3 + i - 1, at(0, 0, i),
        )

    def plane_gather(k, j):
        return remote(pj.at[k, t], pj.at[k, t], pg_sem, k * PEERS + j, plane_peer(j))

    def z_step(k, d, s):
        cols = pl.ds(d * HALF, HALF) if s == 0 else pl.ds(0, FFL)
        return remote(
            zs.at[k, d, s, :, cols], zr.at[k, d, s, :, cols], z_sem, (k * 2 + d) * 4 + s,
            at(1 if d == 0 else -1),
        )

    def a_step(k, d, s):
        piece = lax.rem(z + (NZ - s if d == 0 else s), NZ)
        cols = pl.ds(d * HALF, HALF) if s == 3 else pl.ds(0, FFL)
        ref = dir_v.at[k, c, piece, :, cols]
        return remote(ref, ref, a_sem, (k * 2 + d) * 4 + s, at(1 if d == 0 else -1))

    def sib(k, n):
        ref = dir_v.at[k, c, lax.rem(z + NZ - n, NZ)]
        return remote(ref, ref, sib_sem, k * NZ + n, sibling)

    def stage_x1(k):
        for h in range(2):
            for i in (1, 2, 3):
                start(x1(k, h, i))

    def stage_x2(k):
        for h in range(2):
            for i in (1, 2, 3):
                x1(k, h, i).wait_recv()
            own = part[k, 0, :, pl.ds(x, 1)].reshape(NY, 32, NR) if h == 0 else part[k, 1, y]
            s1[k, h] = own + r1[k, h, 0] + r1[k, h, 1] + r1[k, h, 2]
            for i in (1, 2, 3):
                start(x2(k, h, i))

    def stage_pg(k):
        for h in range(2):
            for i in (1, 2, 3):
                x2(k, h, i).wait_recv()
            own = s1[k, h, y if h == 0 else x]
            pj[k, t, h] = (own + r2[k, h, 0] + r2[k, h, 1] + r2[k, h, 2]).astype(BF16)

        @pl.loop(1, PEERS)
        def _(j):
            plane_gather(k, j).start()

        def drain():
            @pl.loop(1, PEERS)
            def _(j):
                plane_gather(k, j).wait_send()

        drains.append(drain)

    def stage_grad(k):
        @pl.loop(1, PEERS)
        def _(j):
            plane_gather(k, j).wait_recv()

        if k == 0:
            loads[2].wait()
            go_copy.wait_recv()
        pjt[...] = pj[k].reshape(PEERS * 64, NR).T

        value = jnp.dot(pjt[...], go_v[...].reshape(PEERS * 64, FFL), preferred_element_type=F32)
        gp[k] = value.reshape(NZ, RB, FFL)

        for d in range(2):
            far = lax.rem(z + 4, NZ)
            cols = slice(d * HALF, (d + 1) * HALF)
            zs[k, d, 0, :, cols] = gp[k, far, :, cols].astype(BF16)
            start(z_step(k, d, 0))

    def stage_z(k, s):
        for d in range(2):
            z_step(k, d, s - 1).wait_recv()
            dest = lax.rem(z + (4 - s if d == 0 else NZ - 4 + s), NZ)
            if s == 1:
                got = slice(d * HALF, (d + 1) * HALF)
                rest = slice((1 - d) * HALF, (2 - d) * HALF)
                zs[k, d, 1, :, got] = (
                    gp[k, dest, :, got] + zr[k, d, 0, :, got].astype(F32)
                ).astype(BF16)
                zs[k, d, 1, :, rest] = gp[k, dest, :, rest].astype(BF16)
            else:
                zs[k, d, s] = (gp[k, dest] + zr[k, d, s - 1].astype(F32)).astype(BF16)
            start(z_step(k, d, s))

    def stage_adam(k):
        for d in range(2):
            z_step(k, d, 3).wait_recv()
        if k == 0:
            loads[3].wait()
            loads[4].wait()
        rows = slice(k * RB, (k + 1) * RB)
        grad = gp[k, z] + zr[k, 0, 3].astype(F32) + zr[k, 1, 3].astype(F32)
        new_first = 0.9 * first_v[rows, :] + 0.1 * grad
        new_second = 0.999 * second_v[rows, :] + 0.001 * grad * grad
        out_first[rows, :] = new_first
        out_second[rows, :] = new_second
        first_fix = 1.0 - 0.9**STEP
        second_fix = 1.0 - 0.999**STEP
        dir_v[k, c, z] = (
            new_first / first_fix / (jnp.sqrt(new_second / second_fix) + 1e-08)
        ).astype(BF16)
        for d in range(2):
            start(a_step(k, d, 0))
        start(sib(k, 0))

    def stage_a(k, s):
        for d in range(2):
            a_step(k, d, s - 1).wait_recv()
            start(a_step(k, d, s))
            start(sib(k, s if d == 0 else NZ - s))

    def stage_last(k):
        for d in range(2):
            a_step(k, d, 3).wait_recv()
        start(sib(k, 4))

    def stage_product(k):
        for n in range(NZ):
            sib(k, n).wait_recv()

        value = jnp.dot(
            hp[:, k * 2 * NR : (k + 1) * 2 * NR],
            dir_v[k].reshape(2 * NR, FFL),
            preferred_element_type=F32,
        )
        out_w[...] = out_w[...] - 0.5 * value

    holder = dp
    is_holder = t == holder

    def piece_of(ref, p):
        return ref.at[pl.ds(pl.multiple_of(p * 32, 32), 32)]

    def scatter(p):
        return pltpu.make_async_remote_copy(
            src_ref=piece_of(proj_v, p), dst_ref=piece_of(held, p),
            send_sem=sc_sem[0].at[p], recv_sem=sc_sem[1].at[0],
            device_id=(dp, p), device_id_type=MESH,
        )

    def held_gather(j):
        return remote(piece_of(held, t), piece_of(held, t), hg_sem, j, plane_peer(j))

    def own_held():
        return pltpu.make_async_copy(proj_v, held, load_sem.at[6])

    def stage_scatter():
        @pl.when(is_holder)
        def _():
            own_held().start()

            @pl.loop(1, PEERS)
            def _(j):
                scatter(lax.rem(t + j, PEERS)).start()

        def drain():
            @pl.when(is_holder)
            def _():
                @pl.loop(1, PEERS)
                def _(j):
                    scatter(lax.rem(t + j, PEERS)).wait_send()

        drains.append(drain)

    def stage_held_gather():
        @pl.when(is_holder)
        def _():
            own_held().wait()

        @pl.when(jnp.logical_not(is_holder))
        def _():
            scatter(t).wait_recv()

        @pl.loop(1, PEERS)
        def _(j):
            @pl.when(plane_peer(j)[1] != holder)
            def _():
                held_gather(j).start()

        def drain():
            @pl.loop(1, PEERS)
            def _(j):
                @pl.when(plane_peer(j)[1] != holder)
                def _():
                    held_gather(j).wait_send()

        drains.append(drain)

    def stage_held():
        @pl.when(jnp.logical_not(is_holder))
        def _():
            @pl.loop(1, PEERS)
            def _(j):
                held_gather(j).wait_recv()

        for cc in range(2):
            @pl.loop(0, 4)
            def _(b):
                rows = pl.ds(pl.multiple_of(b * 128, 128), 128)
                value = jnp.dot(held[rows, :], pick[cc], preferred_element_type=F32).astype(BF16)
                for k in range(K):
                    lo = (k * 2 + cc) * NR
                    hp[rows, lo : lo + NR] = value[:, k * NR : (k + 1) * NR]

        loads[5].wait()

    tok_copy.wait_recv()
    partial_product(1 - c)

    stages = [
        stage_x1, stage_x2, stage_pg, stage_grad,
        functools.partial(lambda s, k: stage_z(k, s), 1),
        functools.partial(lambda s, k: stage_z(k, s), 2),
        functools.partial(lambda s, k: stage_z(k, s), 3),
        stage_adam,
        functools.partial(lambda s, k: stage_a(k, s), 1),
        functools.partial(lambda s, k: stage_a(k, s), 2),
        functools.partial(lambda s, k: stage_a(k, s), 3),
        stage_last, stage_product,
    ]
    held_stages = {"scatter": stage_scatter, "gather": stage_held_gather, "held": stage_held}
    for item in ORDER:
        if isinstance(item, str):
            held_stages[item]()
        else:
            stages[item[0]](item[1])

    for drain in drains:
        drain()


def on_device(tokens, grad_out, projector, weight, first_moment, second_moment):
    dma = pltpu.SemaphoreType.DMA

    def pair(n):
        return [dma((n,)), dma((n,))]

    scratch = [
        pltpu.VMEM((2, 512, 512), BF16),
        pltpu.VMEM((PEERS, 2, 32, FFL), BF16),
        pltpu.VMEM((512, 1024), BF16),
        pltpu.VMEM((ROWS, FFL), F32),
        pltpu.VMEM((ROWS, FFL), F32),
        pltpu.VMEM((2, 1024, K * NR), BF16),
        pltpu.VMEM((512, K * NR), BF16),
        pltpu.VMEM((K, 2, NY, NX, 32, NR), F32),
        pltpu.VMEM((K, 2, 3, 4, 32, NR), F32),
        pltpu.VMEM((K, 2, 4, 32, NR), F32),
        pltpu.VMEM((K, 2, 3, 32, NR), F32),
        pltpu.VMEM((K, PEERS, 2, 32, NR), BF16),
        pltpu.VMEM((NR, PEERS * 64), BF16),
        pltpu.VMEM((K, NZ, RB, FFL), F32),
        pltpu.VMEM((K, 2, 4, RB, FFL), BF16),
        pltpu.VMEM((K, 2, 4, RB, FFL), BF16),
        pltpu.VMEM((K, 2, NZ, RB, FFL), BF16),
        pltpu.VMEM((512, 1024), BF16),
        pltpu.VMEM((512, 1024), BF16),
        dma((7,)),
        pair(1), pair(1), pair(K * 6), pair(K * 6), pair(K * PEERS), pair(K * 8), pair(K * 8),
        pair(K * NZ), pair(PEERS), pair(PEERS),
    ]
    any_spec = pl.BlockSpec(memory_space=pl.ANY)
    vmem_spec = pl.BlockSpec(memory_space=pltpu.VMEM)
    return pl.pallas_call(
        kernel,
        out_shape=(
            pltpu.VMEM(weight.shape, F32),
            pltpu.VMEM(first_moment.shape, F32),
            pltpu.VMEM(second_moment.shape, F32),
        ),
        in_specs=[any_spec] * 6,
        out_specs=[vmem_spec] * 3,
        scratch_shapes=scratch,
        compiler_params=pltpu.CompilerParams(
            collective_id=0, has_side_effects=True, vmem_limit_bytes=50 * 2**20
        ),
        cost_estimate=pl.CostEstimate(
            flops=6 * 10**9, bytes_accessed=13 * 2**20, transcendentals=0
        ),
    )(tokens, grad_out.reshape(PEERS, 32, FFL), projector, weight, first_moment, second_moment)


def solution(mesh):
    spec = P("dp", "tensor")
    in_specs = (spec, spec, P("tensor", None), spec, spec, spec)
    return jax.shard_map(
        on_device, mesh=mesh, in_specs=in_specs, out_specs=(spec, spec, spec), check_vma=False
    )
```

```python
import functools

import jax
import jax.numpy as jnp
from jax import lax
from jax.experimental import pallas as pl
from jax.experimental.pallas import tpu as pltpu
from jax.sharding import PartitionSpec as P

STEP = 1000
MESH = pl.DeviceIdType.MESH
F32, BF16 = jnp.float32, jnp.bfloat16
K = 4
NZ, NY, NX = 8, 4, 4
ROWS = 64
RB = ROWS // K
NR = NZ * RB
FFL = 1792
HALF = FFL // 2
FAR = ((pl.ds(0, 512), pl.ds(512, 384)), (pl.ds(896, 384), pl.ds(1280, 512)))
PEERS = NY * NX

ORDER = (
    (0, 0), (0, 1), (0, 2), "tok", "pp", (1, 0), (1, 2), "go", (1, 1), (2, 0), (1, 3), (0, 3), (2, 1), (2, 2),
    (3, 0), (2, 3), (3, 1), (3, 2), (4, 0), (3, 3), (4, 1), "scatter", (5, 0), (4, 2), (5, 1), (6, 0), (4, 3),
    (5, 2), (6, 1), (5, 3), (6, 2), "gather", (7, 1), (7, 0), (6, 3), (7, 2), (8, 1), (7, 3), (8, 0), (8, 2),
    (9, 1), (8, 3), (9, 2), (10, 1), (9, 0), (9, 3), (10, 2), (11, 1), (10, 0), "held", (10, 3), (12, 1),
    (11, 2), (11, 0), (11, 3), (12, 2), (13, 1), (12, 0), (13, 2), (12, 3), (13, 0), (13, 3),
)


def kernel(
    tokens, grad_out, projector, weight, first, second,
    out_w, out_first, out_second,
    tok_v, go_v, proj_v, first_v, second_v, pick, pc, part, r1, s1, r2, pj, pjt, gp,
    zs, zr, dir_v, held, hp,
    load_sem, tok_sem, go_sem, x1_sem, x2_sem, pg_sem, z_sem, a_sem, sib_sem, sc_sem, hg_sem,
):
    dp, t = lax.axis_index("dp"), lax.axis_index("tensor")
    z, c = dp // 2, dp % 2
    y, x = t // NX, t % NX

    def at(dz=0, dy=0, dx=0):
        return (lax.rem(z + dz + NZ, NZ) * 2 + c, lax.rem(y + dy, NY) * NX + lax.rem(x + dx, NX))

    sibling = (2 * z + 1 - c, t)

    def plane_peer(j):
        return at(0, j // NX, j % NX)

    def remote(src, dst, sems, idx, device):
        send, recv = sems
        return pltpu.make_async_remote_copy(
            src_ref=src, dst_ref=dst, send_sem=send.at[idx], recv_sem=recv.at[idx],
            device_id=device, device_id_type=MESH,
        )

    drains, seen = [], set()

    def start(copy):
        copy.start()
        drains.append(copy.wait_send)

    barrier = pltpu.get_barrier_semaphore()
    for dz in (1, -1):
        pl.semaphore_signal(barrier, inc=1, device_id=at(dz), device_id_type=MESH)
    pl.semaphore_signal(barrier, inc=1, device_id=sibling, device_id_type=MESH)

    @pl.loop(1, PEERS)
    def _(j):
        pl.semaphore_signal(barrier, inc=1, device_id=plane_peer(j), device_id_type=MESH)

    loads = [
        pltpu.make_async_copy(projector, proj_v, load_sem.at[0]),
        pltpu.make_async_copy(tokens, tok_v.at[c], load_sem.at[1]),
        pltpu.make_async_copy(grad_out, go_v.at[:, c], load_sem.at[2]),
        pltpu.make_async_copy(first, first_v, load_sem.at[3]),
        pltpu.make_async_copy(second, second_v, load_sem.at[4]),
        pltpu.make_async_copy(weight, out_w, load_sem.at[5]),
    ]
    for copy in loads:
        copy.start()

    col = lax.broadcasted_iota(jnp.int32, (1, K * NR), 1)
    natural = col // RB % NZ * (2 * ROWS) + col // NR * RB + col % RB

    @pl.loop(0, NZ)
    def _(b):
        row = lax.broadcasted_iota(jnp.int32, (2 * ROWS, K * NR), 0)
        for cc in range(2):
            hit = row == natural + (cc * ROWS - b * (2 * ROWS))
            pick[cc, pl.ds(pl.multiple_of(b * 2 * ROWS, 2 * ROWS), 2 * ROWS), :] = jnp.where(
                hit, 1.0, 0.0
            ).astype(BF16)

    loads[0].wait()
    pc[...] = jnp.dot(proj_v[...], pick[c], preferred_element_type=F32).astype(BF16)
    loads[1].wait()

    def partial_product(h):
        value = jnp.dot(tok_v[h], pc[...], preferred_element_type=F32)
        for k in range(K):
            part[k, h] = value[:, k * NR : (k + 1) * NR].reshape(NY, NX, 32, NR)

    partial_product(c)

    pl.semaphore_wait(barrier, 2 + 1 + PEERS - 1)
    tok_copy = remote(tok_v.at[c], tok_v.at[c], tok_sem, 0, sibling)
    go_copy = remote(grad_out, go_v.at[:, c], go_sem, 0, sibling)

    def x1(k, h, i):
        if h == 0:
            return remote(
                part.at[k, 0, :, lax.rem(x + i, NX)], r1.at[k, 0, i - 1], x1_sem,
                (k * 2 + h) * 3 + i - 1, at(0, 0, i),
            )
        return remote(
            part.at[k, 1, lax.rem(y + i, NY)], r1.at[k, 1, i - 1], x1_sem,
            (k * 2 + h) * 3 + i - 1, at(0, i, 0),
        )

    def x2(k, h, i):
        if h == 0:
            return remote(
                s1.at[k, 0, lax.rem(y + i, NY)], r2.at[k, 0, i - 1], x2_sem,
                (k * 2 + h) * 3 + i - 1, at(0, i, 0),
            )
        return remote(
            s1.at[k, 1, lax.rem(x + i, NX)], r2.at[k, 1, i - 1], x2_sem,
            (k * 2 + h) * 3 + i - 1, at(0, 0, i),
        )

    def plane_gather(k, j):
        return remote(pj.at[k, t], pj.at[k, t], pg_sem, k * PEERS + j, plane_peer(j))

    def columns(q, s, far_step, d):
        return FAR[q][d] if s == far_step else pl.ds(q * HALF, HALF)

    def z_step(k, d, s, q):
        cols = columns(q, s, 0, d)
        return remote(
            zs.at[k, d, s, :, cols], zr.at[k, d, s, :, cols], z_sem, ((k * 2 + d) * 4 + s) * 2 + q,
            at(1 if d == 0 else -1),
        )

    def a_step(k, d, s, q):
        piece = lax.rem(z + (NZ - s if d == 0 else s), NZ)
        ref = dir_v.at[k, c, piece, :, columns(q, s, 3, d)]
        return remote(ref, ref, a_sem, ((k * 2 + d) * 4 + s) * 2 + q, at(1 if d == 0 else -1))

    def sib(k, n):
        ref = dir_v.at[k, c, lax.rem(z + NZ - n, NZ)]
        return remote(ref, ref, sib_sem, k * NZ + n, sibling)

    def send_half(k, core_of_half):
        for h in range(2):
            @pl.when(core_of_half == h)
            def _():
                for i in (1, 2, 3):
                    x1(k, h, i).start()

            for i in (1, 2, 3):
                if core_of_half is c:
                    drains.append(x1(k, h, i).wait_send)

    def stage_own_half(k):
        send_half(k, c)

    def stage_other_half(k):
        send_half(k, 1 - c)

    def stage_swap_tokens():
        start(tok_copy)

    def stage_other_partial():
        tok_copy.wait_recv()
        partial_product(1 - c)

    def stage_swap_grad():
        start(go_copy)

    def stage_x2(k):
        for h in range(2):
            for i in (1, 2, 3):
                x1(k, h, i).wait_recv()
            own = part[k, 0, :, pl.ds(x, 1)].reshape(NY, 32, NR) if h == 0 else part[k, 1, y]
            s1[k, h] = own + r1[k, h, 0] + r1[k, h, 1] + r1[k, h, 2]
            for i in (1, 2, 3):
                start(x2(k, h, i))

    def stage_pg(k):
        for h in range(2):
            for i in (1, 2, 3):
                x2(k, h, i).wait_recv()
            own = s1[k, h, y if h == 0 else x]
            pj[k, t, h] = (own + r2[k, h, 0] + r2[k, h, 1] + r2[k, h, 2]).astype(BF16)

        @pl.loop(1, PEERS)
        def _(j):
            plane_gather(k, j).start()

        def drain():
            @pl.loop(1, PEERS)
            def _(j):
                plane_gather(k, j).wait_send()

        drains.append(drain)

    def stage_grad(k):
        @pl.loop(1, PEERS)
        def _(j):
            plane_gather(k, j).wait_recv()

        if "grad" not in seen:
            seen.add("grad")
            loads[2].wait()
            go_copy.wait_recv()
        pjt[...] = pj[k].reshape(PEERS * 64, NR).T

        value = jnp.dot(pjt[...], go_v[...].reshape(PEERS * 64, FFL), preferred_element_type=F32)
        gp[k] = value.reshape(NZ, RB, FFL)

        far = lax.rem(z + 4, NZ)
        for q in range(2):
            for d in range(2):
                cols = FAR[q][d]
                zs[k, d, 0, :, cols] = gp[k, far, :, cols].astype(BF16)
                start(z_step(k, d, 0, q))

    def stage_z(k, s):
        for q in range(2):
            half = pl.ds(q * HALF, HALF)
            for d in range(2):
                z_step(k, d, s - 1, q).wait_recv()
                dest = lax.rem(z + (4 - s if d == 0 else NZ - 4 + s), NZ)
                if s == 1:
                    got, rest = FAR[q][d], FAR[q][1 - d]
                    zs[k, d, 1, :, got] = (
                        gp[k, dest, :, got] + zr[k, d, 0, :, got].astype(F32)
                    ).astype(BF16)
                    zs[k, d, 1, :, rest] = gp[k, dest, :, rest].astype(BF16)
                else:
                    zs[k, d, s, :, half] = (
                        gp[k, dest, :, half] + zr[k, d, s - 1, :, half].astype(F32)
                    ).astype(BF16)
                start(z_step(k, d, s, q))

    def stage_adam(k):
        if "adam" not in seen:
            seen.add("adam")
            loads[3].wait()
            loads[4].wait()
        rows = slice(k * RB, (k + 1) * RB)
        first_fix = 1.0 - 0.9**STEP
        second_fix = 1.0 - 0.999**STEP
        for q in range(2):
            half = pl.ds(q * HALF, HALF)
            for d in range(2):
                z_step(k, d, 3, q).wait_recv()
            grad = (
                gp[k, z, :, half] + zr[k, 0, 3, :, half].astype(F32) + zr[k, 1, 3, :, half].astype(F32)
            )
            new_first = 0.9 * first_v[rows, half] + 0.1 * grad
            new_second = 0.999 * second_v[rows, half] + 0.001 * grad * grad
            out_first[rows, half] = new_first
            out_second[rows, half] = new_second
            dir_v[k, c, z, :, half] = (
                new_first / first_fix / (jnp.sqrt(new_second / second_fix) + 1e-08)
            ).astype(BF16)
            for d in range(2):
                start(a_step(k, d, 0, q))
        start(sib(k, 0))

    def stage_a(k, s):
        for q in range(2):
            for d in range(2):
                a_step(k, d, s - 1, q).wait_recv()
                start(a_step(k, d, s, q))
        for n in (s, NZ - s):
            start(sib(k, n))

    def stage_last(k):
        for q in range(2):
            for d in range(2):
                a_step(k, d, 3, q).wait_recv()
        start(sib(k, 4))

    def stage_product(k):
        for n in range(NZ):
            sib(k, n).wait_recv()

        value = jnp.dot(
            hp[:, k * 2 * NR : (k + 1) * 2 * NR],
            dir_v[k].reshape(2 * NR, FFL),
            preferred_element_type=F32,
        )
        out_w[...] = out_w[...] - 0.5 * value

    holder = dp
    is_holder = t == holder

    def piece_of(ref, p):
        return ref.at[pl.ds(pl.multiple_of(p * 32, 32), 32)]

    def scatter(p):
        return pltpu.make_async_remote_copy(
            src_ref=piece_of(proj_v, p), dst_ref=piece_of(held, p),
            send_sem=sc_sem[0].at[p], recv_sem=sc_sem[1].at[0],
            device_id=(dp, p), device_id_type=MESH,
        )

    def held_gather(j):
        return remote(piece_of(held, t), piece_of(held, t), hg_sem, j, plane_peer(j))

    def own_held():
        return pltpu.make_async_copy(proj_v, held, load_sem.at[6])

    def stage_scatter():
        @pl.when(is_holder)
        def _():
            own_held().start()

            @pl.loop(1, PEERS)
            def _(j):
                scatter(lax.rem(t + j, PEERS)).start()

        def drain():
            @pl.when(is_holder)
            def _():
                @pl.loop(1, PEERS)
                def _(j):
                    scatter(lax.rem(t + j, PEERS)).wait_send()

        drains.append(drain)

    def stage_held_gather():
        @pl.when(is_holder)
        def _():
            own_held().wait()

        @pl.when(jnp.logical_not(is_holder))
        def _():
            scatter(t).wait_recv()

        @pl.loop(1, PEERS)
        def _(j):
            @pl.when(plane_peer(j)[1] != holder)
            def _():
                held_gather(j).start()

        def drain():
            @pl.loop(1, PEERS)
            def _(j):
                @pl.when(plane_peer(j)[1] != holder)
                def _():
                    held_gather(j).wait_send()

        drains.append(drain)

    def stage_held():
        @pl.when(jnp.logical_not(is_holder))
        def _():
            @pl.loop(1, PEERS)
            def _(j):
                held_gather(j).wait_recv()

        for cc in range(2):
            value = jnp.dot(held[...], pick[cc], preferred_element_type=F32).astype(BF16)
            for k in range(K):
                lo = (k * 2 + cc) * NR
                hp[:, lo : lo + NR] = value[:, k * NR : (k + 1) * NR]

        loads[5].wait()

    stages = [
        stage_own_half, stage_other_half, stage_x2, stage_pg, stage_grad,
        functools.partial(lambda s, k: stage_z(k, s), 1),
        functools.partial(lambda s, k: stage_z(k, s), 2),
        functools.partial(lambda s, k: stage_z(k, s), 3),
        stage_adam,
        functools.partial(lambda s, k: stage_a(k, s), 1),
        functools.partial(lambda s, k: stage_a(k, s), 2),
        functools.partial(lambda s, k: stage_a(k, s), 3),
        stage_last, stage_product,
    ]
    once = {
        "tok": stage_swap_tokens, "pp": stage_other_partial, "go": stage_swap_grad,
        "scatter": stage_scatter, "gather": stage_held_gather, "held": stage_held,
    }
    for item in ORDER:
        if isinstance(item, str):
            once[item]()
        else:
            stages[item[0]](item[1])

    for drain in drains:
        drain()


def on_device(tokens, grad_out, projector, weight, first_moment, second_moment):
    dma = pltpu.SemaphoreType.DMA

    def pair(n):
        return [dma((n,)), dma((n,))]

    scratch = [
        pltpu.VMEM((2, 512, 512), BF16),
        pltpu.VMEM((PEERS, 2, 32, FFL), BF16),
        pltpu.VMEM((512, 1024), BF16),
        pltpu.VMEM((ROWS, FFL), F32),
        pltpu.VMEM((ROWS, FFL), F32),
        pltpu.VMEM((2, 1024, K * NR), BF16),
        pltpu.VMEM((512, K * NR), BF16),
        pltpu.VMEM((K, 2, NY, NX, 32, NR), F32),
        pltpu.VMEM((K, 2, 3, 4, 32, NR), F32),
        pltpu.VMEM((K, 2, 4, 32, NR), F32),
        pltpu.VMEM((K, 2, 3, 32, NR), F32),
        pltpu.VMEM((K, PEERS, 2, 32, NR), BF16),
        pltpu.VMEM((NR, PEERS * 64), BF16),
        pltpu.VMEM((K, NZ, RB, FFL), F32),
        pltpu.VMEM((K, 2, 4, RB, FFL), BF16),
        pltpu.VMEM((K, 2, 4, RB, FFL), BF16),
        pltpu.VMEM((K, 2, NZ, RB, FFL), BF16),
        pltpu.VMEM((512, 1024), BF16),
        pltpu.VMEM((512, 1024), BF16),
        dma((7,)),
        pair(1), pair(1), pair(K * 6), pair(K * 6), pair(K * PEERS), pair(K * 16), pair(K * 16),
        pair(K * NZ), pair(PEERS), pair(PEERS),
    ]
    any_spec = pl.BlockSpec(memory_space=pl.ANY)
    vmem_spec = pl.BlockSpec(memory_space=pltpu.VMEM)
    return pl.pallas_call(
        kernel,
        out_shape=(
            pltpu.VMEM(weight.shape, F32),
            pltpu.VMEM(first_moment.shape, F32),
            pltpu.VMEM(second_moment.shape, F32),
        ),
        in_specs=[any_spec] * 6,
        out_specs=[vmem_spec] * 3,
        scratch_shapes=scratch,
        compiler_params=pltpu.CompilerParams(
            collective_id=0, has_side_effects=True, vmem_limit_bytes=50 * 2**20
        ),
        cost_estimate=pl.CostEstimate(
            flops=6 * 10**9, bytes_accessed=13 * 2**20, transcendentals=0
        ),
    )(tokens, grad_out.reshape(PEERS, 32, FFL), projector, weight, first_moment, second_moment)


def solution(mesh):
    spec = P("dp", "tensor")
    in_specs = (spec, spec, P("tensor", None), spec, spec, spec)
    return jax.shard_map(
        on_device, mesh=mesh, in_specs=in_specs, out_specs=(spec, spec, spec), check_vma=False
    )
```

```python
import functools

import jax
import jax.numpy as jnp
from jax import lax
from jax.experimental import pallas as pl
from jax.experimental.pallas import tpu as pltpu
from jax.sharding import PartitionSpec as P

STEP = 1000
MESH = pl.DeviceIdType.MESH
F32, BF16 = jnp.float32, jnp.bfloat16
K = 4
NZ, NY, NX = 8, 4, 4
ROWS = 64
RB = ROWS // K
NR = NZ * RB
FFL = 1792
HALF = FFL // 2
LAST = 3
BLOCKS = 4
FAR = ((pl.ds(0, 512), pl.ds(512, 384)), (pl.ds(896, 384), pl.ds(1280, 512)))
PEERS = NY * NX

ORDER = (
    (0, 0), (0, 1), (0, 2), "tok", "pp", (1, 0), (1, 2), "go", (1, 1), (2, 0), (1, 3), (0, 3), (2, 1), (2, 2),
    (3, 0), (2, 3), (3, 1), (3, 2), (4, 0), (3, 3), (4, 1), "scatter", (5, 0), (4, 2), (5, 1), (6, 0), (4, 3),
    (5, 2), (6, 1), (5, 3), (6, 2), "gather", (7, 1), (7, 0), (6, 3), (7, 2), (8, 1), (7, 3), (8, 0), (8, 2),
    (9, 1), (8, 3), (9, 2), (10, 1), (9, 0), (9, 3), (10, 2), (11, 1), (10, 0), (10, 3), (12, 1), (11, 2),
    (11, 0), (11, 3), "held", (12, 2), (13, 1), (12, 0), (13, 2), (12, 3), (13, 0), (13, 3),
)


def kernel(
    tokens, grad_out, projector, weight, first, second,
    out_w, out_first, out_second, dir_v, hp,
    tok_v, go_v, proj_v, first_v, second_v, pick, pc, part, r1, s1, r2, pj, pjt, gp,
    zs, zr, held,
    load_sem, tok_sem, go_sem, x1_sem, x2_sem, pg_sem, z_sem, a_sem, sib_sem, sc_sem, hg_sem,
):
    dp, t = lax.axis_index("dp"), lax.axis_index("tensor")
    z, c = dp // 2, dp % 2
    y, x = t // NX, t % NX

    def at(dz=0, dy=0, dx=0):
        return (lax.rem(z + dz + NZ, NZ) * 2 + c, lax.rem(y + dy, NY) * NX + lax.rem(x + dx, NX))

    sibling = (2 * z + 1 - c, t)

    def plane_peer(j):
        return at(0, j // NX, j % NX)

    def remote(src, dst, sems, idx, device):
        send, recv = sems
        return pltpu.make_async_remote_copy(
            src_ref=src, dst_ref=dst, send_sem=send.at[idx], recv_sem=recv.at[idx],
            device_id=device, device_id_type=MESH,
        )

    drains, seen = [], set()

    def start(copy):
        copy.start()
        drains.append(copy.wait_send)

    barrier = pltpu.get_barrier_semaphore()
    for dz in (1, -1):
        pl.semaphore_signal(barrier, inc=1, device_id=at(dz), device_id_type=MESH)
    pl.semaphore_signal(barrier, inc=1, device_id=sibling, device_id_type=MESH)

    @pl.loop(1, PEERS)
    def _(j):
        pl.semaphore_signal(barrier, inc=1, device_id=plane_peer(j), device_id_type=MESH)

    loads = [
        pltpu.make_async_copy(projector, proj_v, load_sem.at[0]),
        pltpu.make_async_copy(tokens, tok_v.at[c], load_sem.at[1]),
        pltpu.make_async_copy(grad_out, go_v.at[:, c], load_sem.at[2]),
        pltpu.make_async_copy(first, first_v, load_sem.at[3]),
        pltpu.make_async_copy(second, second_v, load_sem.at[4]),
        pltpu.make_async_copy(weight, out_w, load_sem.at[5]),
    ]
    for copy in loads:
        copy.start()

    col = lax.broadcasted_iota(jnp.int32, (1, K * NR), 1)
    natural = col // RB % NZ * (2 * ROWS) + col // NR * RB + col % RB

    @pl.loop(0, NZ)
    def _(b):
        row = lax.broadcasted_iota(jnp.int32, (2 * ROWS, K * NR), 0)
        for cc in range(2):
            hit = row == natural + (cc * ROWS - b * (2 * ROWS))
            pick[cc, pl.ds(pl.multiple_of(b * 2 * ROWS, 2 * ROWS), 2 * ROWS), :] = jnp.where(
                hit, 1.0, 0.0
            ).astype(BF16)

    loads[0].wait()
    pc[...] = jnp.dot(proj_v[...], pick[c], preferred_element_type=F32).astype(BF16)
    loads[1].wait()

    def partial_product(h):
        value = jnp.dot(tok_v[h], pc[...], preferred_element_type=F32)
        for k in range(K):
            part[k, h] = value[:, k * NR : (k + 1) * NR].reshape(NY, NX, 32, NR)

    partial_product(c)

    pl.semaphore_wait(barrier, 2 + 1 + PEERS - 1)
    tok_copy = remote(tok_v.at[c], tok_v.at[c], tok_sem, 0, sibling)
    go_copy = remote(grad_out, go_v.at[:, c], go_sem, 0, sibling)

    def x1(k, h, i):
        if h == 0:
            return remote(
                part.at[k, 0, :, lax.rem(x + i, NX)], r1.at[k, 0, i - 1], x1_sem,
                (k * 2 + h) * 3 + i - 1, at(0, 0, i),
            )
        return remote(
            part.at[k, 1, lax.rem(y + i, NY)], r1.at[k, 1, i - 1], x1_sem,
            (k * 2 + h) * 3 + i - 1, at(0, i, 0),
        )

    def x2(k, h, i):
        if h == 0:
            return remote(
                s1.at[k, 0, lax.rem(y + i, NY)], r2.at[k, 0, i - 1], x2_sem,
                (k * 2 + h) * 3 + i - 1, at(0, i, 0),
            )
        return remote(
            s1.at[k, 1, lax.rem(x + i, NX)], r2.at[k, 1, i - 1], x2_sem,
            (k * 2 + h) * 3 + i - 1, at(0, 0, i),
        )

    def plane_gather(k, j):
        return remote(pj.at[k, t], pj.at[k, t], pg_sem, k * PEERS + j, plane_peer(j))

    def columns(q, s, far_step, d):
        return FAR[q][d] if s == far_step else pl.ds(q * HALF, HALF)

    def z_step(k, d, s, q):
        cols = columns(q, s, 0, d)
        return remote(
            zs.at[k, d, s, :, cols], zr.at[k, d, s, :, cols], z_sem, ((k * 2 + d) * 4 + s) * 2 + q,
            at(1 if d == 0 else -1),
        )

    def a_step(k, d, s, q):
        piece = lax.rem(z + (NZ - s if d == 0 else s), NZ)
        ref = dir_v.at[k, c, piece, :, columns(q, s, 3, d)]
        return remote(ref, ref, a_sem, ((k * 2 + d) * 4 + s) * 2 + q, at(1 if d == 0 else -1))

    def sib(k, n):
        ref = dir_v.at[k, c, lax.rem(z + NZ - n, NZ)]
        return remote(ref, ref, sib_sem, k * NZ + n, sibling)

    def send_half(k, core_of_half):
        for h in range(2):
            @pl.when(core_of_half == h)
            def _():
                for i in (1, 2, 3):
                    x1(k, h, i).start()

            for i in (1, 2, 3):
                if core_of_half is c:
                    drains.append(x1(k, h, i).wait_send)

    def stage_own_half(k):
        send_half(k, c)

    def stage_other_half(k):
        send_half(k, 1 - c)

    def stage_swap_tokens():
        start(tok_copy)

    def stage_other_partial():
        tok_copy.wait_recv()
        partial_product(1 - c)

    def stage_swap_grad():
        start(go_copy)

    def stage_x2(k):
        for h in range(2):
            for i in (1, 2, 3):
                x1(k, h, i).wait_recv()
            own = part[k, 0, :, pl.ds(x, 1)].reshape(NY, 32, NR) if h == 0 else part[k, 1, y]
            s1[k, h] = own + r1[k, h, 0] + r1[k, h, 1] + r1[k, h, 2]
            for i in (1, 2, 3):
                start(x2(k, h, i))

    def stage_pg(k):
        for h in range(2):
            for i in (1, 2, 3):
                x2(k, h, i).wait_recv()
            own = s1[k, h, y if h == 0 else x]
            pj[k, t, h] = (own + r2[k, h, 0] + r2[k, h, 1] + r2[k, h, 2]).astype(BF16)

        @pl.loop(1, PEERS)
        def _(j):
            plane_gather(k, j).start()

        def drain():
            @pl.loop(1, PEERS)
            def _(j):
                plane_gather(k, j).wait_send()

        drains.append(drain)

    def stage_grad(k):
        @pl.loop(1, PEERS)
        def _(j):
            plane_gather(k, j).wait_recv()

        if "grad" not in seen:
            seen.add("grad")
            loads[2].wait()
            go_copy.wait_recv()
        pjt[...] = pj[k].reshape(PEERS * 64, NR).T

        value = jnp.dot(pjt[...], go_v[...].reshape(PEERS * 64, FFL), preferred_element_type=F32)
        gp[k] = value.reshape(NZ, RB, FFL)

        far = lax.rem(z + 4, NZ)
        for q in range(2):
            for d in range(2):
                cols = FAR[q][d]
                zs[k, d, 0, :, cols] = gp[k, far, :, cols].astype(BF16)
                start(z_step(k, d, 0, q))

    def stage_z(k, s):
        for q in range(2):
            half = pl.ds(q * HALF, HALF)
            for d in range(2):
                z_step(k, d, s - 1, q).wait_recv()
                dest = lax.rem(z + (4 - s if d == 0 else NZ - 4 + s), NZ)
                if s == 1:
                    got, rest = FAR[q][d], FAR[q][1 - d]
                    zs[k, d, 1, :, got] = (
                        gp[k, dest, :, got] + zr[k, d, 0, :, got].astype(F32)
                    ).astype(BF16)
                    zs[k, d, 1, :, rest] = gp[k, dest, :, rest].astype(BF16)
                else:
                    zs[k, d, s, :, half] = (
                        gp[k, dest, :, half] + zr[k, d, s - 1, :, half].astype(F32)
                    ).astype(BF16)
                start(z_step(k, d, s, q))

    def stage_adam(k):
        if "adam" not in seen:
            seen.add("adam")
            loads[3].wait()
            loads[4].wait()
        rows = slice(k * RB, (k + 1) * RB)
        first_fix = 1.0 - 0.9**STEP
        second_fix = 1.0 - 0.999**STEP
        for q in range(2):
            half = pl.ds(q * HALF, HALF)
            for d in range(2):
                z_step(k, d, 3, q).wait_recv()
            grad = (
                gp[k, z, :, half] + zr[k, 0, 3, :, half].astype(F32) + zr[k, 1, 3, :, half].astype(F32)
            )
            new_first = 0.9 * first_v[rows, half] + 0.1 * grad
            new_second = 0.999 * second_v[rows, half] + 0.001 * grad * grad
            out_first[rows, half] = new_first
            out_second[rows, half] = new_second
            dir_v[k, c, z, :, half] = (
                new_first / first_fix / (jnp.sqrt(new_second / second_fix) + 1e-08)
            ).astype(BF16)
            for d in range(2):
                start(a_step(k, d, 0, q))
        start(sib(k, 0))

    def stage_a(k, s):
        for q in range(2):
            for d in range(2):
                a_step(k, d, s - 1, q).wait_recv()
                start(a_step(k, d, s, q))
        for n in (s, NZ - s):
            start(sib(k, n))

    def stage_last(k):
        for q in range(2):
            for d in range(2):
                a_step(k, d, 3, q).wait_recv()
        start(sib(k, 4))

    def stage_product(k):
        for n in range(NZ):
            sib(k, n).wait_recv()
        if k == LAST:
            return

        value = jnp.dot(
            hp[:, k * 2 * NR : (k + 1) * 2 * NR],
            dir_v[k].reshape(2 * NR, FFL),
            preferred_element_type=F32,
        )
        out_w[...] = out_w[...] - 0.5 * value

    holder = dp
    is_holder = t == holder

    def piece_of(ref, p):
        return ref.at[pl.ds(pl.multiple_of(p * 32, 32), 32)]

    def scatter(p):
        return pltpu.make_async_remote_copy(
            src_ref=piece_of(proj_v, p), dst_ref=piece_of(held, p),
            send_sem=sc_sem[0].at[p], recv_sem=sc_sem[1].at[0],
            device_id=(dp, p), device_id_type=MESH,
        )

    def held_gather(j):
        return remote(piece_of(held, t), piece_of(held, t), hg_sem, j, plane_peer(j))

    def own_held():
        return pltpu.make_async_copy(proj_v, held, load_sem.at[6])

    def stage_scatter():
        @pl.when(is_holder)
        def _():
            own_held().start()

            @pl.loop(1, PEERS)
            def _(j):
                scatter(lax.rem(t + j, PEERS)).start()

        def drain():
            @pl.when(is_holder)
            def _():
                @pl.loop(1, PEERS)
                def _(j):
                    scatter(lax.rem(t + j, PEERS)).wait_send()

        drains.append(drain)

    def stage_held_gather():
        @pl.when(is_holder)
        def _():
            own_held().wait()

        @pl.when(jnp.logical_not(is_holder))
        def _():
            scatter(t).wait_recv()

        @pl.loop(1, PEERS)
        def _(j):
            @pl.when(plane_peer(j)[1] != holder)
            def _():
                held_gather(j).start()

        def drain():
            @pl.loop(1, PEERS)
            def _(j):
                @pl.when(plane_peer(j)[1] != holder)
                def _():
                    held_gather(j).wait_send()

        drains.append(drain)

    def stage_held():
        @pl.when(jnp.logical_not(is_holder))
        def _():
            @pl.loop(1, PEERS)
            def _(j):
                held_gather(j).wait_recv()

        for cc in range(2):
            value = jnp.dot(held[...], pick[cc], preferred_element_type=F32).astype(BF16)
            for k in range(K):
                lo = (k * 2 + cc) * NR
                hp[:, lo : lo + NR] = value[:, k * NR : (k + 1) * NR]

        loads[5].wait()

    stages = [
        stage_own_half, stage_other_half, stage_x2, stage_pg, stage_grad,
        functools.partial(lambda s, k: stage_z(k, s), 1),
        functools.partial(lambda s, k: stage_z(k, s), 2),
        functools.partial(lambda s, k: stage_z(k, s), 3),
        stage_adam,
        functools.partial(lambda s, k: stage_a(k, s), 1),
        functools.partial(lambda s, k: stage_a(k, s), 2),
        functools.partial(lambda s, k: stage_a(k, s), 3),
        stage_last, stage_product,
    ]
    once = {
        "tok": stage_swap_tokens, "pp": stage_other_partial, "go": stage_swap_grad,
        "scatter": stage_scatter, "gather": stage_held_gather, "held": stage_held,
    }
    for item in ORDER:
        if isinstance(item, str):
            once[item]()
        else:
            stages[item[0]](item[1])

    for drain in drains:
        drain()


def finish(weight, first, second, dir_v, hp, out_w, out_first, out_second, done, sem):
    copies = [
        pltpu.make_async_copy(first, out_first, sem.at[BLOCKS]),
        pltpu.make_async_copy(second, out_second, sem.at[BLOCKS + 1]),
    ]
    for copy in copies:
        copy.start()
    size = weight.shape[0] // BLOCKS
    for b in range(BLOCKS):
        rows = pl.ds(b * size, size)
        value = jnp.dot(
            hp[rows, LAST * 2 * NR : (LAST + 1) * 2 * NR],
            dir_v[LAST].reshape(2 * NR, FFL),
            preferred_element_type=F32,
        )
        done[rows, :] = weight[rows, :] - 0.5 * value
        copy = pltpu.make_async_copy(done.at[rows], out_w.at[rows], sem.at[b])
        copy.start()
        copies.append(copy)
    for copy in copies:
        copy.wait()


def on_device(tokens, grad_out, projector, weight, first_moment, second_moment):
    dma = pltpu.SemaphoreType.DMA

    def pair(n):
        return [dma((n,)), dma((n,))]

    scratch = [
        pltpu.VMEM((2, 512, 512), BF16),
        pltpu.VMEM((PEERS, 2, 32, FFL), BF16),
        pltpu.VMEM((512, 1024), BF16),
        pltpu.VMEM((ROWS, FFL), F32),
        pltpu.VMEM((ROWS, FFL), F32),
        pltpu.VMEM((2, 1024, K * NR), BF16),
        pltpu.VMEM((512, K * NR), BF16),
        pltpu.VMEM((K, 2, NY, NX, 32, NR), F32),
        pltpu.VMEM((K, 2, 3, 4, 32, NR), F32),
        pltpu.VMEM((K, 2, 4, 32, NR), F32),
        pltpu.VMEM((K, 2, 3, 32, NR), F32),
        pltpu.VMEM((K, PEERS, 2, 32, NR), BF16),
        pltpu.VMEM((NR, PEERS * 64), BF16),
        pltpu.VMEM((K, NZ, RB, FFL), F32),
        pltpu.VMEM((K, 2, 4, RB, FFL), BF16),
        pltpu.VMEM((K, 2, 4, RB, FFL), BF16),
        pltpu.VMEM((512, 1024), BF16),
        dma((7,)),
        pair(1), pair(1), pair(K * 6), pair(K * 6), pair(K * PEERS), pair(K * 16), pair(K * 16),
        pair(K * NZ), pair(PEERS), pair(PEERS),
    ]
    any_spec = pl.BlockSpec(memory_space=pl.ANY)
    vmem_spec = pl.BlockSpec(memory_space=pltpu.VMEM)
    values = pl.pallas_call(
        kernel,
        out_shape=(
            pltpu.VMEM(weight.shape, F32),
            pltpu.VMEM(first_moment.shape, F32),
            pltpu.VMEM(second_moment.shape, F32),
            pltpu.VMEM((K, 2, NZ, RB, FFL), BF16),
            pltpu.VMEM((512, 1024), BF16),
        ),
        in_specs=[any_spec] * 6,
        out_specs=[vmem_spec] * 5,
        scratch_shapes=scratch,
        compiler_params=pltpu.CompilerParams(
            collective_id=0, has_side_effects=True, vmem_limit_bytes=103 * 2**19
        ),
        cost_estimate=pl.CostEstimate(
            flops=6 * 10**9, bytes_accessed=13 * 2**20, transcendentals=0
        ),
    )(tokens, grad_out.reshape(PEERS, 32, FFL), projector, weight, first_moment, second_moment)
    return pl.pallas_call(
        finish,
        out_shape=tuple(
            jax.ShapeDtypeStruct(a.shape, F32) for a in (weight, first_moment, second_moment)
        ),
        in_specs=[vmem_spec] * 5,
        out_specs=[any_spec] * 3,
        scratch_shapes=[pltpu.VMEM(weight.shape, F32), dma((BLOCKS + 2,))],
        compiler_params=pltpu.CompilerParams(vmem_limit_bytes=44 * 2**20),
        cost_estimate=pl.CostEstimate(
            flops=470 * 10**6, bytes_accessed=5 * 2**20, transcendentals=0
        ),
    )(*values)


def solution(mesh):
    spec = P("dp", "tensor")
    in_specs = (spec, spec, P("tensor", None), spec, spec, spec)
    return jax.shard_map(
        on_device, mesh=mesh, in_specs=in_specs, out_specs=(spec, spec, spec), check_vma=False
    )
```
